32 devices in a mesh: dp: 8 (over z, y), ctx: 4 (over x, core).
Axes of the slice: x: 2, y: 2, z: 4, core: 2. Of those that a mesh axis runs over, the one named last changes fastest.
Arguments:
- query_rows: bfloat16 [4096, 2048], P(('dp', 'ctx')), may hold values from -6 to 6
- key_rows: bfloat16 [4096, 2048], P(('dp', 'ctx')), may hold values from -6 to 6
- value_rows: bfloat16 [4096, 2048], P(('dp', 'ctx')), may hold values from -6 to 6
- target: bfloat16 [4096, 1536], P(('dp', 'ctx')), may hold values from -18 to 18
- w_out: bfloat16 [2048, 1536], replicated, may hold values from -0.125 to 0.125
- clip_lengths: int32 [8, 4], P('dp'), may hold values from 1 to 256, 512 in all within a row
- timesteps: int32 [8, 4], P('dp'), may hold values from 0 to 999
- tile_pattern: int32 [8, 4, 4], P('dp'), may hold values 0 or 1
- tau_prev: float32 [1], replicated, may hold values from 1 to 4
Outputs:
- query_grad: bfloat16 [4096, 2048], P(('dp', 'ctx'))
- key_grad: bfloat16 [4096, 2048], P(('dp', 'ctx'))
- value_grad: bfloat16 [4096, 2048], P(('dp', 'ctx'))
- weight_grad: float32 [2048, 1536], P('ctx', 'dp')
The draws below stay inside these ranges and needn't reach their ends.
Inputs may be any that keep to these rules, and one draw needn't show every extreme that they name: `clip_lengths`: each row of clip lengths sums to 512, and its largest entry is 256.
All inputs are finite; a program needn't handle non-finite values. No bound on the sum of `tile_pattern` on one device may be relied on, other than what follows from the above.
Results may differ from the reference program's by a relative error of at most 0.019.
Values may be sent and summed in bfloat16 or wider, within the bound.
A program may use at most 128 MiB of HBM per device.

```python
import math
import jax
import jax.numpy as jnp
import numpy as np
from jax import lax

HEADS = 16
HD = 128
OUT = 1536
CLIPS = 4
TILE = 128
DA = 2048
GROUP = 512
TOKENS = 4096
NT = 4
N_DP = 8


def drawn_rows(key, salt):
    return jnp.clip(jax.random.normal(jax.random.fold_in(key, salt), (TOKENS, DA), jnp.float32), -6.0, 6.0)


def draw_query_rows(key, part):
    return drawn_rows(key, 11).astype(jnp.bfloat16)


def draw_key_rows(key, part):
    return drawn_rows(key, 12).astype(jnp.bfloat16)


def draw_target(key, part):
    pack_ids = (jnp.arange(TOKENS, dtype=jnp.int32) // GROUP).astype(jnp.float32)
    fraction = pack_ids / max(N_DP - 1, 1)
    base = jnp.clip(jax.random.normal(jax.random.fold_in(key, 22), (TOKENS, OUT), jnp.float32), -6.0, 6.0)
    ramp = 1.0 + 2.0 * fraction
    return (base * ramp[:, None]).astype(jnp.bfloat16)


def with_ends(values, key, least, high):
    longest = values.shape.index(max(values.shape))
    spots = []
    for shift in (0, 1):
        where = [jax.random.randint(jax.random.fold_in(key, axis), (), 0, length) for axis, length in enumerate(values.shape)]
        where[longest] = (where[longest] + shift) % values.shape[longest]
        spots.append(tuple(where))
    return values.at[spots[0]].set(least).at[spots[1]].set(high)


def steps_of(stream_key, shape, cuts, smallest, top_value):
    def one(axis_at, parts):
        draws = jax.random.uniform(jax.random.fold_in(jax.random.fold_in(stream_key, 6), axis_at), (parts,), jnp.float32, smallest / len(cuts), top_value / len(cuts))
        return jnp.repeat(jnp.exp(draws), shape[axis_at] // parts).reshape((-1,) + (1,) * (len(shape) - axis_at - 1))

    level = one(*cuts[0])
    for cut in cuts[1:]:
        level = level * one(*cut)
    return level


def split_up(amount, total, reach, lean):
    loads = [(1 << 20) // math.isqrt(grade ** lean) + 1 for grade in range(2, amount + 1)]
    surplus, given = total - reach - (amount - 1), [1] * (amount - 1)
    while surplus > 0:
        free = [i for i in range(amount - 1) if given[i] < reach]
        whole, remaining = sum([loads[i] for i in free]), surplus
        for i in free:
            extra = min(reach - given[i], max(1, remaining * loads[i] // whole), surplus)
            given[i] = given[i] + extra
            surplus = surplus - extra
    return np.array([reach] + given)


def ragged_sizes(key, amount, total, reach, lean):
    if amount == 2:
        one = jax.random.randint(key, (), max(1, total - reach), min(reach, total - 1) + 1)
        return jnp.stack([one, total - one])
    lengths = jnp.asarray(split_up(amount, total, reach, lean), jnp.int32)
    pairs = (amount - 1) // 2
    source_of, receiver = lengths[1:1 + 2 * pairs:2], lengths[2:2 + 2 * pairs:2]
    room = jnp.minimum(source_of - 1, reach - receiver)
    moved = jax.random.randint(jax.random.fold_in(key, 1), (pairs,), 0, 1 << 20) % (room + 1)
    lengths = lengths.at[1:1 + 2 * pairs:2].set(source_of - moved).at[2:2 + 2 * pairs:2].set(receiver + moved)
    return lengths[jax.random.permutation(jax.random.fold_in(key, 2), amount)]


def noise(stream_key, extent, deviation, reach, pieces=(), held_as=jnp.bfloat16):
    result = deviation * jax.random.normal(stream_key, extent, jnp.float32)
    if pieces:
        result = result * steps_of(stream_key, extent, pieces, -0.22, 0.18)
    return jnp.clip(result, -reach, reach).astype(held_as)


def setup_inputs(seed: int = 0) -> dict:
    splits = jax.random.split(jax.random.key(seed), 10)
    query_rows = draw_query_rows(jax.random.fold_in(splits[9], 71), 0)
    key_rows = draw_key_rows(jax.random.fold_in(splits[9], 71), 0)
    value_rows = noise(splits[2], (TOKENS, DA), 1.0, 6.0, ((0, 32),))
    target = draw_target(jax.random.fold_in(splits[9], 71), 0)
    w_out = noise(splits[4], (DA, OUT), DA ** -0.5, 0.125)
    clip_lengths = jax.vmap(lambda own: ragged_sizes(own, CLIPS, GROUP, GROUP // 2, 2))(jax.random.split(splits[5], N_DP)).reshape((N_DP, CLIPS)).astype(jnp.int32)
    timesteps = with_ends(jax.random.randint(splits[6], (N_DP, CLIPS), 0, 1000), jax.random.fold_in(splits[6], 1), 0, 999).astype(jnp.int32)
    tile_pattern = with_ends((jax.random.randint(splits[7], (N_DP, NT, NT), 0, 2) < 1).astype(jnp.int32), jax.random.fold_in(splits[7], 1), 0, 1)
    tau_prev = jnp.clip(jax.random.uniform(splits[8], (1,), jnp.float32, 1.0, 4.0), 1.0, 4.0)
    return dict(query_rows=query_rows, key_rows=key_rows, value_rows=value_rows, target=target, w_out=w_out, clip_lengths=clip_lengths, timesteps=timesteps, tile_pattern=tile_pattern, tau_prev=tau_prev)


MOMENTUM = 0.9

def clip_index(lengths_row, positions):
    ends = jnp.cumsum(lengths_row)
    return lax.optimization_barrier(jnp.sum((positions[:, None] >= ends[None, :]).astype(jnp.int32), axis=1)).astype(jnp.int32)

def attention_mask(clip_ids, pattern, row_total):
    tiles = row_total // TILE
    tile_ok = jnp.broadcast_to(pattern[:, None, :, None], (tiles, TILE, tiles, TILE)).reshape(row_total, row_total) > 0
    tile_ids = jnp.arange(row_total, dtype=jnp.int32) // TILE
    same_tile = tile_ids[:, None] == tile_ids[None, :]
    return (clip_ids[:, None] == clip_ids[None, :]) & (tile_ok | same_tile)

def head_probs(query_head, key_head, allowed):
    score_scale = 1.0 / math.sqrt(HD)
    scores = lax.dot_general(query_head, key_head, (((1,), (1,)), ((), ())), preferred_element_type=jnp.float32) * score_scale
    scores = jnp.where(allowed, scores, -1e+30)
    row_max = lax.optimization_barrier(jnp.max(scores, axis=1))
    unnorm = jnp.where(allowed, jnp.exp(scores - row_max[:, None]), 0.0)
    row_total = lax.optimization_barrier(jnp.sum(unnorm, axis=1))
    return unnorm / row_total[:, None]

def head_backward(query_head, key_head, value_head, out_head, grad_head, allowed):
    score_scale = 1.0 / math.sqrt(HD)
    probs = head_probs(query_head, key_head, allowed)
    probs_low = probs.astype(jnp.bfloat16)
    value_grad = lax.dot_general(probs_low, grad_head, (((0,), (0,)), ((), ())), preferred_element_type=jnp.float32).astype(jnp.bfloat16)
    prob_grad = lax.dot_general(grad_head, value_head, (((1,), (1,)), ((), ())), preferred_element_type=jnp.float32)
    delta = lax.optimization_barrier(jnp.sum(grad_head.astype(jnp.float32) * out_head.astype(jnp.float32), axis=1))
    score_grad = (probs * (prob_grad - delta[:, None])).astype(jnp.bfloat16)
    query_grad = (jnp.dot(score_grad, key_head, preferred_element_type=jnp.float32) * score_scale).astype(jnp.bfloat16)
    key_grad = (lax.dot_general(score_grad, query_head, (((0,), (0,)), ((), ())), preferred_element_type=jnp.float32) * score_scale).astype(jnp.bfloat16)
    return (query_grad, key_grad, value_grad)

def superloss_weight(clip_loss, tau_now):
    argument = jnp.maximum(-0.3, 0.5 * (clip_loss - tau_now))
    branch = jnp.log1p(argument)
    for sweep in range(5):
        exp_value = jnp.exp(branch)
        branch = branch - (branch * exp_value - argument) / (exp_value * (branch + 1.0))
    return jnp.exp(-branch)

def reference(query_rows, key_rows, value_rows, target, w_out, clip_lengths, timesteps, tile_pattern, tau_prev):
    positions = jnp.arange(GROUP, dtype=jnp.int32)
    clip_all = jax.vmap(lambda lengths_row: clip_index(lengths_row, positions))(clip_lengths)
    query_pack = query_rows.reshape(N_DP, GROUP, DA)
    key_pack = key_rows.reshape(N_DP, GROUP, DA)
    value_pack = value_rows.reshape(N_DP, GROUP, DA)

    def forward(inputs):
        query_one, key_one, value_one, clip_one, pattern_one = inputs
        allowed = attention_mask(clip_one, pattern_one, GROUP)
        head_outs = []
        for head in range(HEADS):
            cols = slice(head * HD, (head + 1) * HD)
            probs = head_probs(query_one[:, cols], key_one[:, cols], allowed)
            head_outs.append(jnp.dot(probs.astype(jnp.bfloat16), value_one[:, cols], preferred_element_type=jnp.float32).astype(jnp.bfloat16))
        return jnp.concatenate(head_outs, axis=1)
    attended = lax.map(forward, (query_pack, key_pack, value_pack, clip_all, tile_pattern)).reshape(TOKENS, DA)
    predicted = jnp.dot(attended, w_out, preferred_element_type=jnp.float32)
    residue = predicted - target.astype(jnp.float32)
    row_squares = lax.optimization_barrier(jnp.sum(residue * residue, axis=1)).reshape(N_DP, GROUP)
    onehot = (clip_all[:, :, None] == jnp.arange(CLIPS, dtype=jnp.int32)[None, None, :]).astype(jnp.float32)
    clip_sq = lax.optimization_barrier(jnp.sum(row_squares[:, :, None] * onehot, axis=1))
    clip_len = clip_lengths.astype(jnp.float32)
    step_weight = 1.0 + timesteps.astype(jnp.float32) / 250.0
    clip_loss = step_weight * clip_sq / (clip_len * OUT)
    loss_mean = jnp.sum(clip_loss) / (N_DP * CLIPS)
    tau_now = MOMENTUM * tau_prev[0] + (1.0 - MOMENTUM) * loss_mean
    confidence = superloss_weight(clip_loss, tau_now)
    clip_scale = confidence * step_weight
    row_scale = lax.optimization_barrier(jnp.sum(onehot * clip_scale[:, None, :], axis=2)).reshape(TOKENS)
    pred_grad = (residue * row_scale[:, None]).astype(jnp.bfloat16)
    weight_grad = lax.dot_general(attended, pred_grad, (((0,), (0,)), ((), ())), preferred_element_type=jnp.float32) * (1.0 / math.sqrt(TOKENS))
    attended_grad = lax.dot_general(pred_grad, w_out, (((1,), (1,)), ((), ())), preferred_element_type=jnp.float32).astype(jnp.bfloat16)

    def backward(inputs):
        query_one, key_one, value_one, out_one, grad_one, clip_one, pattern_one = inputs
        allowed = attention_mask(clip_one, pattern_one, GROUP)
        parts_q, parts_k, parts_v = ([], [], [])
        for head in range(HEADS):
            cols = slice(head * HD, (head + 1) * HD)
            grads = head_backward(query_one[:, cols], key_one[:, cols], value_one[:, cols], out_one[:, cols], grad_one[:, cols], allowed)
            parts_q.append(grads[0])
            parts_k.append(grads[1])
            parts_v.append(grads[2])
        return (jnp.concatenate(parts_q, axis=1), jnp.concatenate(parts_k, axis=1), jnp.concatenate(parts_v, axis=1))
    query_grad, key_grad, value_grad = lax.map(backward, (query_pack, key_pack, value_pack, attended.reshape(N_DP, GROUP, DA), attended_grad.reshape(N_DP, GROUP, DA), clip_all, tile_pattern))
    return (query_grad.reshape(TOKENS, DA), key_grad.reshape(TOKENS, DA), value_grad.reshape(TOKENS, DA), weight_grad)
```

```python
import functools
import math

import jax
import jax.numpy as jnp
from jax import lax
from jax.experimental import pallas as pl
from jax.experimental.pallas import tpu as pltpu
from jax.sharding import PartitionSpec as P

HD = 128
OUT = 1536
CLIPS = 4
TILE = 128
MOMENTUM = 0.9
F32 = jnp.float32
BF16 = jnp.bfloat16
CHUNK = 512


def dot_nt(a, b):
    return lax.dot_general(a, b, (((1,), (1,)), ((), ())), preferred_element_type=F32)


def dot_nn(a, b):
    return jnp.dot(a, b, preferred_element_type=F32)


def dot_tn(a, b):
    return lax.dot_general(a, b, (((0,), (0,)), ((), ())), preferred_element_type=F32)


def superloss_weight(clip_loss, tau_now):
    argument = jnp.maximum(-0.3, 0.5 * (clip_loss - tau_now))
    branch = jnp.log1p(argument)
    for sweep in range(5):
        exp_value = jnp.exp(branch)
        branch = branch - (branch * exp_value - argument) / (exp_value * (branch + 1.0))
    return jnp.exp(-branch)


def kernel(
    C, NY, NZ, RB, DA,
    q_in, k_in, v_in, tgt_in, w_in, len_s, time_s, pat_s, tau_s,
    qg, kg, vg, wg,
    qh, kh, vh, bias, probs, oh, osc, orow, w_v, tgt_v, respack, graw, gh,
    dqh, dkh, dvh, wt, yrecv, zsend, zrecv, wacc, lsend, lctx, ly, lz,
    local_sem, in_send, in_recv, out_send, out_recv, lc_send, lc_recv, ly_send, ly_recv,
    lz_send, lz_recv, res_send, res_recv, rel_send, rel_recv, wy_send, wy_recv, wz_send, wz_recv,
    gr_send, gr_recv, own_sem,
):
    PR = RB * C
    WD = DA // C
    H = WD // HD
    X = C // 2
    DP = NY * NZ
    B = OUT // DP
    NT = PR // TILE
    NCH = OUT // CHUNK
    me = lax.axis_index("ctx")
    dp = lax.axis_index("dp")
    xi, core = me // 2, lax.rem(me, 2)
    zi, yi = dp // NY, lax.rem(dp, NY)
    sib = xi * 2 + (1 - core)

    def ctx_peer(o):
        return lax.rem(me + o, C)

    def ctx_src(o):
        return lax.rem(me + C - o, C)

    def x_peer(o):
        return lax.rem(xi + o, X) * 2 + core

    def y_dev(o):
        return zi * NY + lax.rem(yi + o, NY)

    def z_dev(k):
        return lax.rem(zi + k, NZ) * NY + yi

    def rows(p, n=RB):
        return pl.ds(pl.multiple_of(p * n, n), n)

    def cols(base, h):
        return pl.ds(pl.multiple_of(base + h * HD, HD), HD)

    def remote(src, dst, ss, rs, where):
        return pltpu.make_async_remote_copy(
            src_ref=src, dst_ref=dst, send_sem=ss, recv_sem=rs,
            device_id=where, device_id_type=pl.DeviceIdType.MESH,
        )

    ins, heads_in = (q_in, k_in, v_in), (qh, kh, vh)
    grads_h, grads_out = (dqh, dkh, dvh), (qg, kg, vg)

    def local_in(t):
        return pltpu.make_async_copy(
            ins[t].at[:, pl.ds(pl.multiple_of(me * WD, WD), WD)], heads_in[t].at[rows(me), :],
            local_sem.at[t])

    copy_t = pltpu.make_async_copy(tgt_in, tgt_v, local_sem.at[3])
    copy_w = pltpu.make_async_copy(w_in, w_v, local_sem.at[4])
    for t in range(3):
        local_in(t).start()
    copy_t.start()
    copy_w.start()

    barrier = pltpu.get_barrier_semaphore()
    for o in range(1, C):
        pl.semaphore_signal(barrier, inc=1, device_id={"ctx": ctx_peer(o)},
                            device_id_type=pl.DeviceIdType.MESH)
    for o in range(1, NY):
        pl.semaphore_signal(barrier, inc=1, device_id={"dp": y_dev(o)},
                            device_id_type=pl.DeviceIdType.MESH)
    for k in range(1, NZ):
        pl.semaphore_signal(barrier, inc=1, device_id={"dp": z_dev(k)},
                            device_id_type=pl.DeviceIdType.MESH)
    pl.semaphore_wait(barrier, (C - 1) + (NY - 1) + (NZ - 1))

    def in_copy(t, h, o):
        p = ctx_peer(o)
        return remote(ins[t].at[:, cols(p * WD, h)], heads_in[t].at[rows(me), cols(0, h)],
                      in_send.at[t, h, o], in_recv.at[t, h, o], {"ctx": p})

    @pl.loop(0, H)
    def _(h):
        for o in range(1, C):
            for t in range(3):
                in_copy(t, h, o).start()

    ends = []
    for c in range(CLIPS):
        ends.append(len_s[0, c] if c == 0 else ends[-1] + len_s[0, c])

    def clip_of(pos):
        total = (pos >= ends[0]).astype(jnp.int32)
        for c in range(1, CLIPS):
            total = total + (pos >= ends[c]).astype(jnp.int32)
        return total

    @pl.loop(0, NT)
    def _(i):
        rpos = lax.broadcasted_iota(jnp.int32, (TILE, PR), 0) + i * TILE
        cpos = lax.broadcasted_iota(jnp.int32, (TILE, PR), 1)
        tile = cpos // TILE
        ok = (tile == i).astype(jnp.int32)
        for j in range(NT):
            ok = jnp.where(tile == j, jnp.maximum(ok, pat_s[0, i, j]), ok)
        allowed = (clip_of(rpos) == clip_of(cpos)) & (ok > 0)
        bias[rows(i, TILE), :] = jnp.where(allowed, 0.0, -1e30)

    scale = 1.0 / math.sqrt(HD)
    for t in range(3):
        local_in(t).wait()

    def out_copy(h, o):
        p = ctx_peer(o)
        return remote(oh.at[rows(p), cols(0, h)], orow.at[:, cols(me * WD, h)],
                      out_send.at[h, o], out_recv.at[h, o], {"ctx": p})

    @pl.loop(0, H)
    def _(h):
        for o in range(1, C):
            for t in range(3):
                in_copy(t, h, o).wait_recv()
        k = kh[:, cols(0, h)]
        v = vh[:, cols(0, h)]
        for i in range(NT):
            rr = slice(i * TILE, (i + 1) * TILE)
            s = dot_nt(qh[rr, cols(0, h)], k) * scale + bias[rr, :]
            e = jnp.exp(s - jnp.max(s, axis=1, keepdims=True))
            p = e * (1.0 / jnp.sum(e, axis=1, keepdims=True))
            probs[h, rr, :] = p
            oh[rr, cols(0, h)] = dot_nn(p.astype(BF16), v).astype(BF16)
        for o in range(1, C):
            out_copy(h, o).start()
        orow[:, cols(me * WD, h)] = oh[rows(me), cols(0, h)]

    copy_t.wait()
    copy_w.wait()

    @pl.loop(0, H)
    def _(h):
        for o in range(1, C):
            out_copy(h, o).wait_recv()

    rowsq = jnp.zeros((RB, 1), F32)
    for n in range(NCH):
        cc = slice(n * CHUNK, (n + 1) * CHUNK)
        res = dot_nn(orow[...], w_v[:, cc]) - tgt_v[:, cc].astype(F32)
        rowsq = rowsq + jnp.sum(res * res, axis=1, keepdims=True)
        respack[rows(me), cc] = res.astype(BF16)

    lane = lax.broadcasted_iota(jnp.int32, (RB, 128), 1)
    own_clip = clip_of(lax.broadcasted_iota(jnp.int32, (RB, 128), 0) + me * RB)
    part = jnp.sum(jnp.where(own_clip == lane, rowsq, 0.0), axis=0, keepdims=True)
    lsend[0] = jnp.broadcast_to(part, (8, 128))

    def lctx_copy(o):
        return remote(lsend.at[0], lctx.at[o], lc_send.at[o], lc_recv.at[o], {"ctx": ctx_peer(o)})

    def ly_copy(o):
        return remote(lsend.at[1], ly.at[o], ly_send.at[o], ly_recv.at[o], {"dp": y_dev(o)})

    def lz_copy(k):
        return remote(lsend.at[2], lz.at[k], lz_send.at[k], lz_recv.at[k], {"dp": z_dev(k)})

    for o in range(1, C):
        lctx_copy(o).start()

    def res_view(p, n):
        return respack.at[rows(p), pl.ds(n * CHUNK, CHUNK)]

    def res_copy(n, o):
        p = sib if o == 0 else x_peer(o)
        return remote(res_view(me, n), res_view(me, n), res_send.at[n, o], res_recv.at[n, o],
                      {"ctx": p})

    def relay_copy(n, o):
        p = lax.rem(xi + X - o, X) * 2 + core
        return remote(res_view(p, n), res_view(p, n), rel_send.at[n, o], rel_recv.at[n, o],
                      {"ctx": sib})

    for n in range(NCH):
        for o in range(1, X):
            res_copy(n, o).start()
    for n in range(NCH):
        res_copy(n, 0).start()

    def grad_rows(p):
        graw[rows(p), :] = dot_nt(respack[rows(p), :], w_v[rows(me, WD), :])

    grad_rows(me)
    lanes8 = lax.broadcasted_iota(jnp.int32, (8, 128), 1)
    length = jnp.ones((8, 128), F32)
    weight = jnp.zeros((8, 128), F32)
    for c in range(CLIPS):
        length = jnp.where(lanes8 == c, len_s[0, c].astype(F32), length)
        weight = jnp.where(lanes8 == c, 1.0 + time_s[0, c].astype(F32) / 250.0, weight)
    clip_sq = lsend[0]
    for o in range(1, C):
        lctx_copy(o).wait_recv()
        clip_sq = clip_sq + lctx[o]
    clip_loss = weight * clip_sq / (length * OUT)
    loss_sum = jnp.broadcast_to(jnp.sum(clip_loss, axis=1, keepdims=True), (8, 128))
    lsend[1] = loss_sum
    for o in range(1, NY):
        ly_copy(o).start()

    for n in range(NCH):
        res_copy(n, 0).wait_recv()
    grad_rows(sib)
    for o in range(1, NY):
        ly_copy(o).wait_recv()
        loss_sum = loss_sum + ly[o]
    lsend[2] = loss_sum
    for k in range(1, NZ):
        lz_copy(k).start()

    for n in range(NCH):
        for o in range(1, X):
            res_copy(n, o).wait_recv()
            relay_copy(n, o).start()
    for o in range(1, X):
        grad_rows(lax.rem(xi + X - o, X) * 2 + core)

    for k in range(1, NZ):
        lz_copy(k).wait_recv()
        loss_sum = loss_sum + lz[k]
    tau_now = MOMENTUM * tau_s[0] + (1.0 - MOMENTUM) * (loss_sum / (DP * CLIPS))
    clip_scale = (superloss_weight(clip_loss, tau_now) * weight)[0:1, :]
    norm = 1.0 / math.sqrt(PR * DP)

    def row_scale(i):
        pos = lax.broadcasted_iota(jnp.int32, (RB, 128), 0) + i * RB
        return jnp.sum(jnp.where(clip_of(pos) == lane, clip_scale, 0.0), axis=1, keepdims=True)

    scales = [row_scale(i) for i in range(C)]
    for i in range(C):
        rr = slice(i * RB, (i + 1) * RB)
        osc[rr, :] = (oh[rr, :].astype(F32) * (scales[i] * norm)).astype(BF16)

    for n in range(NCH):
        for o in range(1, X):
            relay_copy(n, o).wait_recv()
    for o in range(1, X):
        grad_rows(lax.rem(xi + X - o, X) * 2 + (1 - core))
    for i in range(C):
        rr = slice(i * RB, (i + 1) * RB)
        gh[rr, :] = (graw[rr, :] * scales[i]).astype(BF16)

    @pl.loop(0, OUT // 256)
    def _(n):
        wt[rows(n, 256), :] = dot_tn(respack[:, rows(n, 256)], osc[...]).astype(BF16)

    def wy_copy(o, k):
        kk = lax.rem(zi + k, NZ)
        return remote(wt.at[rows(kk * NY + lax.rem(yi + o, NY), B), :], yrecv.at[o, lax.rem(k, NZ)],
                      wy_send.at[o, lax.rem(k, NZ)], wy_recv.at[o, lax.rem(k, NZ)],
                      {"dp": y_dev(o)})

    def wz_copy(k):
        return remote(zsend.at[k], zrecv.at[k], wz_send.at[k], wz_recv.at[k], {"dp": z_dev(k)})

    def y_total(k):
        total = wt[rows(lax.rem(zi + k, NZ) * NY + yi, B), :].astype(F32)
        for o in range(1, NY):
            wy_copy(o, k).wait_recv()
            total = total + yrecv[o, lax.rem(k, NZ)].astype(F32)
        return total

    @pl.loop(1, NZ + 1)
    def _(k):
        for o in range(1, NY):
            wy_copy(o, k).start()

    def grad_copy(t, h, o):
        p = ctx_peer(o)
        return remote(grads_h[t].at[rows(p), cols(0, h)], grads_out[t].at[:, cols(me * WD, h)],
                      gr_send.at[t, h, o], gr_recv.at[t, h, o], {"ctx": p})

    def own_grad(t):
        return pltpu.make_async_copy(
            grads_h[t].at[rows(me), :],
            grads_out[t].at[:, pl.ds(pl.multiple_of(me * WD, WD), WD)], own_sem.at[t])

    per_head = -(-NZ // H)

    @pl.loop(0, H)
    def _(h):
        hc = cols(0, h)
        k = kh[:, hc]
        v = vh[:, hc]
        dk_t = jnp.zeros((HD, PR), F32)
        dv_t = jnp.zeros((HD, PR), F32)
        for i in range(NT):
            rr = slice(i * TILE, (i + 1) * TILE)
            g = gh[rr, hc]
            p = probs[h, rr, :]
            gf = g.astype(F32)
            delta = jnp.sum(gf * oh[rr, hc].astype(F32), axis=1, keepdims=True)
            ds = (p * (dot_nt(g, v) - delta)).astype(BF16)
            dqh[rr, hc] = (dot_nn(ds, k) * scale).astype(BF16)
            dk_t = dk_t + dot_nn(qh[rr, hc].T, ds)
            dv_t = dv_t + dot_nn(g.T, p.astype(BF16))
        dkh[:, hc] = (dk_t * scale).T.astype(BF16)
        dvh[:, hc] = dv_t.T.astype(BF16)
        for o in range(1, C):
            for t in range(3):
                grad_copy(t, h, o).start()
        for kk in range(per_head):
            step = h * per_head + kk + 1

            @pl.when(step < NZ)
            def _():
                zsend[step] = y_total(step).astype(BF16)
                wz_copy(step).start()

    for t in range(3):
        own_grad(t).start()
    wacc[...] = y_total(NZ)
    total = wacc[...]
    for k in range(1, NZ):
        wz_copy(k).wait_recv()
        total = total + zrecv[k].astype(F32)
    wg[...] = total.T

    @pl.loop(0, H)
    def _(h):
        for o in range(1, C):
            out_copy(h, o).wait_send()
            for t in range(3):
                in_copy(t, h, o).wait_send()
                grad_copy(t, h, o).wait_send()
                grad_copy(t, h, o).wait_recv()

    for o in range(1, C):
        lctx_copy(o).wait_send()
    for o in range(1, NY):
        ly_copy(o).wait_send()
    for k in range(1, NZ):
        lz_copy(k).wait_send()
        wz_copy(k).wait_send()
    for n in range(NCH):
        for o in range(X):
            res_copy(n, o).wait_send()
        for o in range(1, X):
            relay_copy(n, o).wait_send()

    @pl.loop(1, NZ + 1)
    def _(k):
        for o in range(1, NY):
            wy_copy(o, k).wait_send()

    for t in range(3):
        own_grad(t).wait()


def on_device(
    query_rows, key_rows, value_rows, target, w_out, clip_lengths, timesteps, tile_pattern, tau_prev
):
    RB, DA = query_rows.shape
    C = lax.axis_size("ctx")
    DP = lax.axis_size("dp")
    NY = 2 ** ((DP.bit_length() - 1) // 2)
    NZ = DP // NY
    PR, WD, B = RB * C, DA // C, OUT // DP
    H, X, NCH = WD // HD, C // 2, OUT // CHUNK
    dma = pltpu.SemaphoreType.DMA
    vm = pltpu.VMEM
    anyspec = pl.BlockSpec(memory_space=pl.ANY)
    smem = pl.BlockSpec(memory_space=pltpu.SMEM)
    rows_shape = jax.ShapeDtypeStruct((RB, DA), BF16)
    scratch = [
        vm((PR, WD), BF16), vm((PR, WD), BF16), vm((PR, WD), BF16),
        vm((PR, PR), F32), vm((H, PR, PR), F32), vm((PR, WD), BF16), vm((PR, WD), BF16),
        vm((RB, DA), BF16), vm((DA, OUT), BF16), vm((RB, OUT), BF16), vm((PR, OUT), BF16),
        vm((PR, WD), F32), vm((PR, WD), BF16),
        vm((PR, WD), BF16), vm((PR, WD), BF16), vm((PR, WD), BF16),
        vm((OUT, WD), BF16), vm((NY, NZ, B, WD), BF16), vm((NZ, B, WD), BF16),
        vm((NZ, B, WD), BF16), vm((B, WD), F32),
        vm((3, 8, 128), F32), vm((C, 8, 128), F32), vm((NY, 8, 128), F32), vm((NZ, 8, 128), F32),
        dma((5,)), dma((3, H, C)), dma((3, H, C)), dma((H, C)), dma((H, C)),
        dma((C,)), dma((C,)), dma((NY,)), dma((NY,)), dma((NZ,)), dma((NZ,)),
        dma((NCH, X)), dma((NCH, X)), dma((NCH, X)), dma((NCH, X)),
        dma((NY, NZ)), dma((NY, NZ)), dma((NZ,)), dma((NZ,)),
        dma((3, H, C)), dma((3, H, C)), dma((3,)),
    ]
    return pl.pallas_call(
        functools.partial(kernel, C, NY, NZ, RB, DA),
        out_shape=(rows_shape, rows_shape, rows_shape, jax.ShapeDtypeStruct((WD, B), F32)),
        in_specs=[anyspec] * 5 + [smem] * 4,
        out_specs=(anyspec, anyspec, anyspec, pl.BlockSpec(memory_space=pltpu.VMEM)),
        scratch_shapes=scratch,
        compiler_params=pltpu.CompilerParams(
            collective_id=0, has_side_effects=True, vmem_limit_bytes=56 * 1024 * 1024
        ),
    )(query_rows, key_rows, value_rows, target, w_out, clip_lengths, timesteps, tile_pattern,
      tau_prev)


def solution(mesh):
    return jax.shard_map(
        on_device,
        mesh=mesh,
        in_specs=(
            P(("dp", "ctx"), None),
            P(("dp", "ctx"), None),
            P(("dp", "ctx"), None),
            P(("dp", "ctx"), None),
            P(),
            P("dp", None),
            P("dp", None),
            P("dp", None, None),
            P(),
        ),
        out_specs=(
            P(("dp", "ctx"), None),
            P(("dp", "ctx"), None),
            P(("dp", "ctx"), None),
            P("ctx", "dp"),
        ),
        check_vma=False,
    )
```

```python
import functools
import math

import jax
import jax.numpy as jnp
from jax import lax
from jax.experimental import pallas as pl
from jax.experimental.pallas import tpu as pltpu
from jax.sharding import PartitionSpec as P

HD = 128
OUT = 1536
CLIPS = 4
TILE = 128
MOMENTUM = 0.9
F32 = jnp.float32
BF16 = jnp.bfloat16
CHUNK = 512


def dot_nt(a, b):
    return lax.dot_general(a, b, (((1,), (1,)), ((), ())), preferred_element_type=F32)


def dot_nn(a, b):
    return jnp.dot(a, b, preferred_element_type=F32)


def dot_tn(a, b):
    return lax.dot_general(a, b, (((0,), (0,)), ((), ())), preferred_element_type=F32)


def superloss_weight(clip_loss, tau_now):
    argument = jnp.maximum(-0.3, 0.5 * (clip_loss - tau_now))
    branch = jnp.log1p(argument)
    for sweep in range(5):
        exp_value = jnp.exp(branch)
        branch = branch - (branch * exp_value - argument) / (exp_value * (branch + 1.0))
    return jnp.exp(-branch)


def kernel(
    C, NY, NZ, RB, DA,
    q_in, k_in, v_in, tgt_in, w_in, len_s, time_s, pat_s, tau_s,
    qg, kg, vg, wg,
    qh, kh, vh, bias, probs, oh, osc, orow, w_v, tgt_v, respack, graw, gh,
    dqh, dkh, dvh, wt, yrecv, zsend, zrecv, wacc, lsend, lctx, ly, lz,
    local_sem, in_send, in_recv, out_send, out_recv, lc_send, lc_recv, ly_send, ly_recv,
    lz_send, lz_recv, res_send, res_recv, rel_send, rel_recv, wy_send, wy_recv, wz_send, wz_recv,
    gr_send, gr_recv, own_sem,
):
    PR = RB * C
    WD = DA // C
    H = WD // HD
    X = C // 2
    DP = NY * NZ
    B = OUT // DP
    NT = PR // TILE
    NCH = OUT // CHUNK
    me = lax.axis_index("ctx")
    dp = lax.axis_index("dp")
    xi, core = me // 2, lax.rem(me, 2)
    zi, yi = dp // NY, lax.rem(dp, NY)
    sib = xi * 2 + (1 - core)

    def ctx_peer(o):
        return lax.rem(me + o, C)

    def ctx_src(o):
        return lax.rem(me + C - o, C)

    def x_peer(o):
        return lax.rem(xi + o, X) * 2 + core

    def y_dev(o):
        return zi * NY + lax.rem(yi + o, NY)

    def z_dev(k):
        return lax.rem(zi + k, NZ) * NY + yi

    def rows(p, n=RB):
        return pl.ds(pl.multiple_of(p * n, n), n)

    def cols(base, h):
        return pl.ds(pl.multiple_of(base + h * HD, HD), HD)

    def remote(src, dst, ss, rs, where):
        return pltpu.make_async_remote_copy(
            src_ref=src, dst_ref=dst, send_sem=ss, recv_sem=rs,
            device_id=where, device_id_type=pl.DeviceIdType.MESH,
        )

    ins, heads_in = (q_in, k_in, v_in), (qh, kh, vh)
    grads_h, grads_out = (dqh, dkh, dvh), (qg, kg, vg)

    def local_in(t):
        return pltpu.make_async_copy(
            ins[t].at[:, pl.ds(pl.multiple_of(me * WD, WD), WD)], heads_in[t].at[rows(me), :],
            local_sem.at[t])

    copy_t = pltpu.make_async_copy(tgt_in, tgt_v, local_sem.at[3])
    copy_w = pltpu.make_async_copy(w_in, w_v, local_sem.at[4])
    for t in range(3):
        local_in(t).start()
    copy_t.start()
    copy_w.start()

    barrier = pltpu.get_barrier_semaphore()
    for o in range(1, C):
        pl.semaphore_signal(barrier, inc=1, device_id={"ctx": ctx_peer(o)},
                            device_id_type=pl.DeviceIdType.MESH)
    for o in range(1, NY):
        pl.semaphore_signal(barrier, inc=1, device_id={"dp": y_dev(o)},
                            device_id_type=pl.DeviceIdType.MESH)
    for k in range(1, NZ):
        pl.semaphore_signal(barrier, inc=1, device_id={"dp": z_dev(k)},
                            device_id_type=pl.DeviceIdType.MESH)
    pl.semaphore_wait(barrier, (C - 1) + (NY - 1) + (NZ - 1))

    def in_copy(t, h, o):
        p = ctx_peer(o)
        return remote(ins[t].at[:, cols(p * WD, h)], heads_in[t].at[rows(me), cols(0, h)],
                      in_send.at[t, h, o], in_recv.at[t, h, o], {"ctx": p})

    @pl.loop(0, H)
    def _(h):
        for o in range(1, C):
            for t in range(3):
                in_copy(t, h, o).start()

    ends = []
    for c in range(CLIPS):
        ends.append(len_s[0, c] if c == 0 else ends[-1] + len_s[0, c])

    def clip_of(pos):
        total = (pos >= ends[0]).astype(jnp.int32)
        for c in range(1, CLIPS):
            total = total + (pos >= ends[c]).astype(jnp.int32)
        return total

    @pl.loop(0, NT)
    def _(i):
        rpos = lax.broadcasted_iota(jnp.int32, (TILE, PR), 0) + i * TILE
        cpos = lax.broadcasted_iota(jnp.int32, (TILE, PR), 1)
        tile = cpos // TILE
        ok = (tile == i).astype(jnp.int32)
        for j in range(NT):
            ok = jnp.where(tile == j, jnp.maximum(ok, pat_s[0, i, j]), ok)
        allowed = (clip_of(rpos) == clip_of(cpos)) & (ok > 0)
        bias[rows(i, TILE), :] = jnp.where(allowed, 0.0, -1e30)

    scale = 1.0 / math.sqrt(HD)
    for t in range(3):
        local_in(t).wait()

    def out_copy(h, o):
        p = ctx_peer(o)
        return remote(oh.at[rows(p), cols(0, h)], orow.at[:, cols(me * WD, h)],
                      out_send.at[h, o], out_recv.at[h, o], {"ctx": p})

    @pl.loop(0, H)
    def _(h):
        for o in range(1, C):
            for t in range(3):
                in_copy(t, h, o).wait_recv()
        k = kh[:, cols(0, h)]
        v = vh[:, cols(0, h)]
        for i in range(NT):
            rr = slice(i * TILE, (i + 1) * TILE)
            s = dot_nt(qh[rr, cols(0, h)], k) * scale + bias[rr, :]
            e = jnp.exp(s - jnp.max(s, axis=1, keepdims=True))
            p = e * (1.0 / jnp.sum(e, axis=1, keepdims=True))
            probs[h, rr, :] = p
            oh[rr, cols(0, h)] = dot_nn(p.astype(BF16), v).astype(BF16)
        for o in range(1, C):
            out_copy(h, o).start()
        orow[:, cols(me * WD, h)] = oh[rows(me), cols(0, h)]

    copy_t.wait()
    copy_w.wait()

    @pl.loop(0, H)
    def _(h):
        for o in range(1, C):
            out_copy(h, o).wait_recv()

    def res_view(p, n):
        return respack.at[rows(p), pl.ds(n * CHUNK, CHUNK)]

    def res_copy(n, o):
        p = sib if o == 0 else x_peer(o)
        return remote(res_view(me, n), res_view(me, n), res_send.at[n, o], res_recv.at[n, o],
                      {"ctx": p})

    def relay_copy(n, o):
        p = lax.rem(xi + X - o, X) * 2 + core
        return remote(res_view(p, n), res_view(p, n), rel_send.at[n, o], rel_recv.at[n, o],
                      {"ctx": sib})

    rowsq = jnp.zeros((RB, 1), F32)
    for n in range(NCH):
        cc = slice(n * CHUNK, (n + 1) * CHUNK)
        res = dot_nn(orow[...], w_v[:, cc]) - tgt_v[:, cc].astype(F32)
        rowsq = rowsq + jnp.sum(res * res, axis=1, keepdims=True)
        respack[rows(me), cc] = res.astype(BF16)
        if n < NCH - 1:
            for o in range(1, X):
                res_copy(n, o).start()

    lane = lax.broadcasted_iota(jnp.int32, (RB, 128), 1)
    own_clip = clip_of(lax.broadcasted_iota(jnp.int32, (RB, 128), 0) + me * RB)
    part = jnp.sum(jnp.where(own_clip == lane, rowsq, 0.0), axis=0, keepdims=True)
    lsend[0] = jnp.broadcast_to(part, (8, 128))

    def lctx_copy(o):
        return remote(lsend.at[0], lctx.at[o], lc_send.at[o], lc_recv.at[o], {"ctx": ctx_peer(o)})

    def ly_copy(o):
        return remote(lsend.at[1], ly.at[o], ly_send.at[o], ly_recv.at[o], {"dp": y_dev(o)})

    def lz_copy(k):
        return remote(lsend.at[2], lz.at[k], lz_send.at[k], lz_recv.at[k], {"dp": z_dev(k)})

    for o in range(1, C):
        lctx_copy(o).start()

    for o in range(1, X):
        res_copy(NCH - 1, o).start()
    for n in range(NCH):
        res_copy(n, 0).start()

    def grad_rows(p):
        graw[rows(p), :] = dot_nt(respack[rows(p), :], w_v[rows(me, WD), :])

    grad_rows(me)
    lanes8 = lax.broadcasted_iota(jnp.int32, (8, 128), 1)
    length = jnp.ones((8, 128), F32)
    weight = jnp.zeros((8, 128), F32)
    for c in range(CLIPS):
        length = jnp.where(lanes8 == c, len_s[0, c].astype(F32), length)
        weight = jnp.where(lanes8 == c, 1.0 + time_s[0, c].astype(F32) / 250.0, weight)
    clip_sq = lsend[0]
    for o in range(1, C):
        lctx_copy(o).wait_recv()
        clip_sq = clip_sq + lctx[o]
    clip_loss = weight * clip_sq / (length * OUT)
    loss_sum = jnp.broadcast_to(jnp.sum(clip_loss, axis=1, keepdims=True), (8, 128))
    lsend[1] = loss_sum
    for o in range(1, NY):
        ly_copy(o).start()

    for n in range(NCH):
        res_copy(n, 0).wait_recv()
    grad_rows(sib)
    for o in range(1, NY):
        ly_copy(o).wait_recv()
        loss_sum = loss_sum + ly[o]
    lsend[2] = loss_sum
    for k in range(1, NZ):
        lz_copy(k).start()

    for n in range(NCH):
        for o in range(1, X):
            res_copy(n, o).wait_recv()
            relay_copy(n, o).start()
    for o in range(1, X):
        grad_rows(lax.rem(xi + X - o, X) * 2 + core)

    for k in range(1, NZ):
        lz_copy(k).wait_recv()
        loss_sum = loss_sum + lz[k]
    tau_now = MOMENTUM * tau_s[0] + (1.0 - MOMENTUM) * (loss_sum / (DP * CLIPS))
    clip_scale = (superloss_weight(clip_loss, tau_now) * weight)[0:1, :]
    norm = 1.0 / math.sqrt(PR * DP)

    def row_scale(i):
        pos = lax.broadcasted_iota(jnp.int32, (RB, 128), 0) + i * RB
        return jnp.sum(jnp.where(clip_of(pos) == lane, clip_scale, 0.0), axis=1, keepdims=True)

    scales = [row_scale(i) for i in range(C)]
    for i in range(C):
        rr = slice(i * RB, (i + 1) * RB)
        osc[rr, :] = (oh[rr, :].astype(F32) * (scales[i] * norm)).astype(BF16)

    for n in range(NCH):
        for o in range(1, X):
            relay_copy(n, o).wait_recv()
    def weight_rows(n, width):
        wt[rows(n, width), :] = dot_tn(respack[:, rows(n, width)], osc[...]).astype(BF16)

    def wy_copy(o, k):
        kk = lax.rem(zi + k, NZ)
        return remote(wt.at[rows(kk * NY + lax.rem(yi + o, NY), B), :], yrecv.at[o, lax.rem(k, NZ)],
                      wy_send.at[o, lax.rem(k, NZ)], wy_recv.at[o, lax.rem(k, NZ)],
                      {"dp": y_dev(o)})

    def wz_copy(k):
        return remote(zsend.at[k], zrecv.at[k], wz_send.at[k], wz_recv.at[k], {"dp": z_dev(k)})

    def y_total(k):
        total = wt[rows(lax.rem(zi + k, NZ) * NY + yi, B), :].astype(F32)
        for o in range(1, NY):
            wy_copy(o, k).wait_recv()
            total = total + yrecv[o, lax.rem(k, NZ)].astype(F32)
        return total

    by_z = (NY * B) % 128 == 0
    if not by_z:
        pl.loop(0, OUT // 256)(lambda n: weight_rows(n, 256))

    @pl.loop(1, NZ + 1)
    def _(k):
        if by_z:
            weight_rows(lax.rem(zi + k, NZ), NY * B)
        for o in range(1, NY):
            wy_copy(o, k).start()

    for o in range(1, X):
        grad_rows(lax.rem(xi + X - o, X) * 2 + (1 - core))
    for i in range(C):
        rr = slice(i * RB, (i + 1) * RB)
        gh[rr, :] = (graw[rr, :] * scales[i]).astype(BF16)


    def grad_copy(t, h, o):
        p = ctx_peer(o)
        return remote(grads_h[t].at[rows(p), cols(0, h)], grads_out[t].at[:, cols(me * WD, h)],
                      gr_send.at[t, h, o], gr_recv.at[t, h, o], {"ctx": p})

    def own_grad(t):
        return pltpu.make_async_copy(
            grads_h[t].at[rows(me), :],
            grads_out[t].at[:, pl.ds(pl.multiple_of(me * WD, WD), WD)], own_sem.at[t])

    per_head = -(-NZ // H)

    @pl.loop(0, H)
    def _(h):
        hc = cols(0, h)
        k = kh[:, hc]
        v = vh[:, hc]
        dk_t = jnp.zeros((HD, PR), F32)
        dv_t = jnp.zeros((HD, PR), F32)
        for i in range(NT):
            rr = slice(i * TILE, (i + 1) * TILE)
            g = gh[rr, hc]
            p = probs[h, rr, :]
            gf = g.astype(F32)
            delta = jnp.sum(gf * oh[rr, hc].astype(F32), axis=1, keepdims=True)
            ds = (p * (dot_nt(g, v) - delta)).astype(BF16)
            dqh[rr, hc] = (dot_nn(ds, k) * scale).astype(BF16)
            dk_t = dk_t + dot_nn(qh[rr, hc].T, ds)
            dv_t = dv_t + dot_nn(g.T, p.astype(BF16))
        dkh[:, hc] = (dk_t * scale).T.astype(BF16)
        dvh[:, hc] = dv_t.T.astype(BF16)
        for o in range(1, C):
            for t in range(3):
                grad_copy(t, h, o).start()
        for kk in range(per_head):
            step = h * per_head + kk + 1

            @pl.when(step < NZ)
            def _():
                zsend[step] = y_total(step).astype(BF16)
                wz_copy(step).start()

    for t in range(3):
        own_grad(t).start()
    wacc[...] = y_total(NZ)
    total = wacc[...]
    for k in range(1, NZ):
        wz_copy(k).wait_recv()
        total = total + zrecv[k].astype(F32)
    wg[...] = total

    @pl.loop(0, H)
    def _(h):
        for o in range(1, C):
            out_copy(h, o).wait_send()
            for t in range(3):
                in_copy(t, h, o).wait_send()
                grad_copy(t, h, o).wait_send()
                grad_copy(t, h, o).wait_recv()

    for o in range(1, C):
        lctx_copy(o).wait_send()
    for o in range(1, NY):
        ly_copy(o).wait_send()
    for k in range(1, NZ):
        lz_copy(k).wait_send()
        wz_copy(k).wait_send()
    for n in range(NCH):
        for o in range(X):
            res_copy(n, o).wait_send()
        for o in range(1, X):
            relay_copy(n, o).wait_send()

    @pl.loop(1, NZ + 1)
    def _(k):
        for o in range(1, NY):
            wy_copy(o, k).wait_send()

    for t in range(3):
        own_grad(t).wait()


def place_kernel(*refs):
    half = len(refs) // 2
    sems, sources, results = refs[-1], refs[:half], refs[half:-1]
    copies = []
    for a, (source, result) in enumerate(zip(sources, results)):
        pieces = 4 if source.shape[0] % 64 == 0 else 1
        part = source.shape[0] // pieces
        for j in range(pieces):
            where = pl.ds(j * part, part)
            copies.append(
                pltpu.make_async_copy(source.at[where, :], result.at[where, :], sems.at[a, j]))
    for copy in copies:
        copy.start()
    for copy in copies:
        copy.wait()


def on_device(
    query_rows, key_rows, value_rows, target, w_out, clip_lengths, timesteps, tile_pattern, tau_prev
):
    RB, DA = query_rows.shape
    C = lax.axis_size("ctx")
    DP = lax.axis_size("dp")
    NY = 2 ** ((DP.bit_length() - 1) // 2)
    NZ = DP // NY
    PR, WD, B = RB * C, DA // C, OUT // DP
    H, X, NCH = WD // HD, C // 2, OUT // CHUNK
    dma = pltpu.SemaphoreType.DMA
    vm = pltpu.VMEM
    anyspec = pl.BlockSpec(memory_space=pl.ANY)
    smem = pl.BlockSpec(memory_space=pltpu.SMEM)
    rows_shape = jax.ShapeDtypeStruct((RB, DA), BF16)
    scratch = [
        vm((PR, WD), BF16), vm((PR, WD), BF16), vm((PR, WD), BF16),
        vm((PR, PR), F32), vm((H, PR, PR), F32), vm((PR, WD), BF16), vm((PR, WD), BF16),
        vm((RB, DA), BF16), vm((DA, OUT), BF16), vm((RB, OUT), BF16), vm((PR, OUT), BF16),
        vm((PR, WD), F32), vm((PR, WD), BF16),
        vm((PR, WD), BF16), vm((PR, WD), BF16), vm((PR, WD), BF16),
        vm((OUT, WD), BF16), vm((NY, NZ, B, WD), BF16), vm((NZ, B, WD), BF16),
        vm((NZ, B, WD), BF16), vm((B, WD), F32),
        vm((3, 8, 128), F32), vm((C, 8, 128), F32), vm((NY, 8, 128), F32), vm((NZ, 8, 128), F32),
        dma((5,)), dma((3, H, C)), dma((3, H, C)), dma((H, C)), dma((H, C)),
        dma((C,)), dma((C,)), dma((NY,)), dma((NY,)), dma((NZ,)), dma((NZ,)),
        dma((NCH, X)), dma((NCH, X)), dma((NCH, X)), dma((NCH, X)),
        dma((NY, NZ)), dma((NY, NZ)), dma((NZ,)), dma((NZ,)),
        dma((3, H, C)), dma((3, H, C)), dma((3,)),
    ]
    shapes = (rows_shape, rows_shape, rows_shape, jax.ShapeDtypeStruct((B, WD), F32))
    results = pl.pallas_call(
        functools.partial(kernel, C, NY, NZ, RB, DA),
        out_shape=shapes,
        in_specs=[anyspec] * 5 + [smem] * 4,
        out_specs=(anyspec, anyspec, anyspec, pl.BlockSpec(memory_space=pltpu.VMEM)),
        scratch_shapes=scratch,
        compiler_params=pltpu.CompilerParams(
            collective_id=0, has_side_effects=True, vmem_limit_bytes=56 * 1024 * 1024
        ),
    )(query_rows, key_rows, value_rows, target, w_out, clip_lengths, timesteps, tile_pattern,
      tau_prev)
    query_grad, key_grad, value_grad, weight_grad = pl.pallas_call(
        place_kernel,
        out_shape=shapes,
        in_specs=[anyspec] * 4,
        out_specs=(anyspec,) * 4,
        scratch_shapes=[dma((4, 4))],
        compiler_params=pltpu.CompilerParams(vmem_limit_bytes=56 * 1024 * 1024),
    )(*results)
    return query_grad, key_grad, value_grad, weight_grad.T


def solution(mesh):
    return jax.shard_map(
        on_device,
        mesh=mesh,
        in_specs=(
            P(("dp", "ctx"), None),
            P(("dp", "ctx"), None),
            P(("dp", "ctx"), None),
            P(("dp", "ctx"), None),
            P(),
            P("dp", None),
            P("dp", None),
            P("dp", None, None),
            P(),
        ),
        out_specs=(
            P(("dp", "ctx"), None),
            P(("dp", "ctx"), None),
            P(("dp", "ctx"), None),
            P("ctx", "dp"),
        ),
        check_vma=False,
    )
```

```python
import functools
import math

import jax
import jax.numpy as jnp
from jax import lax
from jax.experimental import pallas as pl
from jax.experimental.pallas import tpu as pltpu
from jax.sharding import PartitionSpec as P

HD = 128
OUT = 1536
CLIPS = 4
TILE = 128
MOMENTUM = 0.9
F32 = jnp.float32
BF16 = jnp.bfloat16
CHUNK = 512


def dot_nt(a, b):
    return lax.dot_general(a, b, (((1,), (1,)), ((), ())), preferred_element_type=F32)


def dot_nn(a, b):
    return jnp.dot(a, b, preferred_element_type=F32)


def dot_tn(a, b):
    return lax.dot_general(a, b, (((0,), (0,)), ((), ())), preferred_element_type=F32)


def superloss_weight(clip_loss, tau_now):
    argument = jnp.maximum(-0.3, 0.5 * (clip_loss - tau_now))
    branch = jnp.log1p(argument)
    for sweep in range(5):
        exp_value = jnp.exp(branch)
        branch = branch - (branch * exp_value - argument) / (exp_value * (branch + 1.0))
    return jnp.exp(-branch)


def kernel(
    C, NY, NZ, RB, DA,
    q_in, k_in, v_in, tgt_in, w_in, len_s, time_s, pat_s, tau_s,
    qg, kg, vg, wg,
    qh, kh, vh, bias, probs, oh, osc, orow, w_v, tgt_v, respack, graw, gh,
    dqh, dkh, dvh, wt, yrecv, zsend, zrecv, wacc, lsend, lctx, ly, lz,
    local_sem, in_send, in_recv, out_send, out_recv, lc_send, lc_recv, ly_send, ly_recv,
    lz_send, lz_recv, res_send, res_recv, rel_send, rel_recv, wy_send, wy_recv, wz_send, wz_recv,
    gr_send, gr_recv, own_sem,
):
    PR = RB * C
    WD = DA // C
    H = WD // HD
    X = C // 2
    DP = NY * NZ
    B = OUT // DP
    NT = PR // TILE
    NCH = OUT // CHUNK
    me = lax.axis_index("ctx")
    dp = lax.axis_index("dp")
    xi, core = me // 2, lax.rem(me, 2)
    zi, yi = dp // NY, lax.rem(dp, NY)
    sib = xi * 2 + (1 - core)

    def ctx_peer(o):
        return lax.rem(me + o, C)

    def ctx_src(o):
        return lax.rem(me + C - o, C)

    def x_peer(o):
        return lax.rem(xi + o, X) * 2 + core

    def y_dev(o):
        return zi * NY + lax.rem(yi + o, NY)

    def z_dev(k):
        return lax.rem(zi + k, NZ) * NY + yi

    def rows(p, n=RB):
        return pl.ds(pl.multiple_of(p * n, n), n)

    def cols(base, h):
        return pl.ds(pl.multiple_of(base + h * HD, HD), HD)

    def remote(src, dst, ss, rs, where):
        return pltpu.make_async_remote_copy(
            src_ref=src, dst_ref=dst, send_sem=ss, recv_sem=rs,
            device_id=where, device_id_type=pl.DeviceIdType.MESH,
        )

    ins, heads_in = (q_in, k_in, v_in), (qh, kh, vh)
    grads_h, grads_out = (dqh, dkh, dvh), (qg, kg, vg)

    def local_in(t):
        return pltpu.make_async_copy(
            ins[t].at[:, pl.ds(pl.multiple_of(me * WD, WD), WD)], heads_in[t].at[rows(me), :],
            local_sem.at[t])

    copy_t = pltpu.make_async_copy(tgt_in, tgt_v, local_sem.at[3])
    copy_w = pltpu.make_async_copy(w_in, w_v, local_sem.at[4])
    for t in range(3):
        local_in(t).start()
    copy_t.start()
    copy_w.start()

    barrier = pltpu.get_barrier_semaphore()
    for o in range(1, C):
        pl.semaphore_signal(barrier, inc=1, device_id={"ctx": ctx_peer(o)},
                            device_id_type=pl.DeviceIdType.MESH)
    for o in range(1, NY):
        pl.semaphore_signal(barrier, inc=1, device_id={"dp": y_dev(o)},
                            device_id_type=pl.DeviceIdType.MESH)
    for k in range(1, NZ):
        pl.semaphore_signal(barrier, inc=1, device_id={"dp": z_dev(k)},
                            device_id_type=pl.DeviceIdType.MESH)
    pl.semaphore_wait(barrier, (C - 1) + (NY - 1) + (NZ - 1))

    def in_copy(t, h, o):
        p = ctx_peer(o)
        return remote(ins[t].at[:, cols(p * WD, h)], heads_in[t].at[rows(me), cols(0, h)],
                      in_send.at[t, h, o], in_recv.at[t, h, o], {"ctx": p})

    @pl.loop(0, H)
    def _(h):
        for o in range(1, C):
            for t in range(3):
                in_copy(t, h, o).start()

    ends = []
    for c in range(CLIPS):
        ends.append(len_s[0, c] if c == 0 else ends[-1] + len_s[0, c])

    def clip_of(pos):
        total = (pos >= ends[0]).astype(jnp.int32)
        for c in range(1, CLIPS):
            total = total + (pos >= ends[c]).astype(jnp.int32)
        return total

    @pl.loop(0, NT)
    def _(i):
        rpos = lax.broadcasted_iota(jnp.int32, (TILE, PR), 0) + i * TILE
        cpos = lax.broadcasted_iota(jnp.int32, (TILE, PR), 1)
        tile = cpos // TILE
        ok = (tile == i).astype(jnp.int32)
        for j in range(NT):
            ok = jnp.where(tile == j, jnp.maximum(ok, pat_s[0, i, j]), ok)
        allowed = (clip_of(rpos) == clip_of(cpos)) & (ok > 0)
        bias[rows(i, TILE), :] = jnp.where(allowed, 0.0, -1e30)

    scale = 1.0 / math.sqrt(HD)
    for t in range(3):
        local_in(t).wait()

    def out_copy(h, o):
        p = ctx_peer(o)
        return remote(oh.at[rows(p), cols(0, h)], orow.at[:, cols(me * WD, h)],
                      out_send.at[h, o], out_recv.at[h, o], {"ctx": p})

    @pl.loop(0, H)
    def _(h):
        for o in range(1, C):
            for t in range(3):
                in_copy(t, h, o).wait_recv()
        k = kh[:, cols(0, h)]
        v = vh[:, cols(0, h)]
        for i in range(NT):
            rr = slice(i * TILE, (i + 1) * TILE)
            s = dot_nt(qh[rr, cols(0, h)], k) * scale + bias[rr, :]
            e = jnp.exp(s - jnp.max(s, axis=1, keepdims=True))
            p = e * (1.0 / jnp.sum(e, axis=1, keepdims=True))
            probs[h, rr, :] = p
            oh[rr, cols(0, h)] = dot_nn(p.astype(BF16), v).astype(BF16)
        for o in range(1, C):
            out_copy(h, o).start()
        orow[:, cols(me * WD, h)] = oh[rows(me), cols(0, h)]

    copy_t.wait()
    copy_w.wait()

    @pl.loop(0, H)
    def _(h):
        for o in range(1, C):
            out_copy(h, o).wait_recv()

    def res_view(p, n):
        return respack.at[rows(p), pl.ds(n * CHUNK, CHUNK)]

    def res_copy(n, o):
        p = sib if o == 0 else x_peer(o)
        return remote(res_view(me, n), res_view(me, n), res_send.at[n, o], res_recv.at[n, o],
                      {"ctx": p})

    def relay_copy(n, o):
        p = lax.rem(xi + X - o, X) * 2 + core
        return remote(res_view(p, n), res_view(p, n), rel_send.at[n, o], rel_recv.at[n, o],
                      {"ctx": sib})

    rowsq = jnp.zeros((RB, 1), F32)
    for n in range(NCH):
        cc = slice(n * CHUNK, (n + 1) * CHUNK)
        res = dot_nn(orow[...], w_v[:, cc]) - tgt_v[:, cc].astype(F32)
        rowsq = rowsq + jnp.sum(res * res, axis=1, keepdims=True)
        respack[rows(me), cc] = res.astype(BF16)
        if n < NCH - 1:
            for o in range(1, X):
                res_copy(n, o).start()

    lane = lax.broadcasted_iota(jnp.int32, (RB, 128), 1)
    own_clip = clip_of(lax.broadcasted_iota(jnp.int32, (RB, 128), 0) + me * RB)
    part = jnp.sum(jnp.where(own_clip == lane, rowsq, 0.0), axis=0, keepdims=True)
    lsend[0] = jnp.broadcast_to(part, (8, 128))

    def lctx_copy(o):
        return remote(lsend.at[0], lctx.at[o], lc_send.at[o], lc_recv.at[o], {"ctx": ctx_peer(o)})

    def ly_copy(o):
        return remote(lsend.at[1], ly.at[o], ly_send.at[o], ly_recv.at[o], {"dp": y_dev(o)})

    def lz_copy(k):
        return remote(lsend.at[2], lz.at[k], lz_send.at[k], lz_recv.at[k], {"dp": z_dev(k)})

    for o in range(1, C):
        lctx_copy(o).start()

    for o in range(1, X):
        res_copy(NCH - 1, o).start()
    for n in range(NCH):
        res_copy(n, 0).start()

    def grad_rows(p):
        graw[rows(p), :] = dot_nt(respack[rows(p), :], w_v[rows(me, WD), :])

    grad_rows(me)
    lanes8 = lax.broadcasted_iota(jnp.int32, (8, 128), 1)
    length = jnp.ones((8, 128), F32)
    weight = jnp.zeros((8, 128), F32)
    for c in range(CLIPS):
        length = jnp.where(lanes8 == c, len_s[0, c].astype(F32), length)
        weight = jnp.where(lanes8 == c, 1.0 + time_s[0, c].astype(F32) / 250.0, weight)
    clip_sq = lsend[0]
    for o in range(1, C):
        lctx_copy(o).wait_recv()
        clip_sq = clip_sq + lctx[o]
    clip_loss = weight * clip_sq / (length * OUT)
    loss_sum = jnp.broadcast_to(jnp.sum(clip_loss, axis=1, keepdims=True), (8, 128))
    lsend[1] = loss_sum
    for o in range(1, NY):
        ly_copy(o).start()

    for n in range(NCH):
        res_copy(n, 0).wait_recv()
    grad_rows(sib)
    for o in range(1, NY):
        ly_copy(o).wait_recv()
        loss_sum = loss_sum + ly[o]
    lsend[2] = loss_sum
    for k in range(1, NZ):
        lz_copy(k).start()

    for n in range(NCH):
        for o in range(1, X):
            res_copy(n, o).wait_recv()
            relay_copy(n, o).start()
    for o in range(1, X):
        grad_rows(lax.rem(xi + X - o, X) * 2 + core)

    for k in range(1, NZ):
        lz_copy(k).wait_recv()
        loss_sum = loss_sum + lz[k]
    tau_now = MOMENTUM * tau_s[0] + (1.0 - MOMENTUM) * (loss_sum / (DP * CLIPS))
    clip_scale = (superloss_weight(clip_loss, tau_now) * weight)[0:1, :]
    norm = 1.0 / math.sqrt(PR * DP)

    def row_scale(i):
        pos = lax.broadcasted_iota(jnp.int32, (RB, 128), 0) + i * RB
        return jnp.sum(jnp.where(clip_of(pos) == lane, clip_scale, 0.0), axis=1, keepdims=True)

    scales = [row_scale(i) for i in range(C)]
    for i in range(C):
        rr = slice(i * RB, (i + 1) * RB)
        osc[rr, :] = (oh[rr, :].astype(F32) * (scales[i] * norm)).astype(BF16)

    for n in range(NCH):
        for o in range(1, X):
            relay_copy(n, o).wait_recv()
    def weight_rows(n, width):
        wt[rows(n, width), :] = dot_tn(respack[:, rows(n, width)], osc[...]).astype(BF16)

    def wy_copy(o, k):
        kk = lax.rem(zi + k, NZ)
        return remote(wt.at[rows(kk * NY + lax.rem(yi + o, NY), B), :], yrecv.at[o, lax.rem(k, NZ)],
                      wy_send.at[o, lax.rem(k, NZ)], wy_recv.at[o, lax.rem(k, NZ)],
                      {"dp": y_dev(o)})

    def wz_copy(k):
        return remote(zsend.at[k], zrecv.at[k], wz_send.at[k], wz_recv.at[k], {"dp": z_dev(k)})

    def y_total(k):
        total = wt[rows(lax.rem(zi + k, NZ) * NY + yi, B), :].astype(F32)
        for o in range(1, NY):
            wy_copy(o, k).wait_recv()
            total = total + yrecv[o, lax.rem(k, NZ)].astype(F32)
        return total

    by_z = (NY * B) % 128 == 0
    if not by_z:
        pl.loop(0, OUT // 256)(lambda n: weight_rows(n, 256))

    @pl.loop(1, NZ + 1)
    def _(k):
        if by_z:
            weight_rows(lax.rem(zi + k, NZ), NY * B)
        for o in range(1, NY):
            wy_copy(o, k).start()

    for o in range(1, X):
        grad_rows(lax.rem(xi + X - o, X) * 2 + (1 - core))
    for i in range(C):
        rr = slice(i * RB, (i + 1) * RB)
        gh[rr, :] = (graw[rr, :] * scales[i]).astype(BF16)


    def grad_copy(t, h, o):
        p = ctx_peer(o)
        return remote(grads_h[t].at[rows(p), cols(0, h)], grads_out[t].at[:, cols(me * WD, h)],
                      gr_send.at[t, h, o], gr_recv.at[t, h, o], {"ctx": p})

    def own_grad(t):
        return pltpu.make_async_copy(
            grads_h[t].at[rows(me), :],
            grads_out[t].at[:, pl.ds(pl.multiple_of(me * WD, WD), WD)], own_sem.at[t])

    per_head = -(-NZ // H)

    @pl.loop(0, H)
    def _(h):
        hc = cols(0, h)
        k = kh[:, hc]
        v = vh[:, hc]
        dk_t = jnp.zeros((HD, PR), F32)
        dv_t = jnp.zeros((HD, PR), F32)
        for i in range(NT):
            rr = slice(i * TILE, (i + 1) * TILE)
            g = gh[rr, hc]
            p = probs[h, rr, :]
            gf = g.astype(F32)
            delta = jnp.sum(gf * oh[rr, hc].astype(F32), axis=1, keepdims=True)
            ds = (p * (dot_nt(g, v) - delta)).astype(BF16)
            dqh[rr, hc] = (dot_nn(ds, k) * scale).astype(BF16)
            dk_t = dk_t + dot_nn(qh[rr, hc].T, ds)
            dv_t = dv_t + dot_nn(g.T, p.astype(BF16))
        dkh[:, hc] = (dk_t * scale).T.astype(BF16)
        dvh[:, hc] = dv_t.T.astype(BF16)
        for o in range(1, C):
            for t in range(3):
                grad_copy(t, h, o).start()
        for kk in range(per_head):
            step = h * per_head + kk + 1

            @pl.when(step < NZ)
            def _():
                zsend[step] = y_total(step).astype(BF16)
                wz_copy(step).start()

    for t in range(3):
        own_grad(t).start()
    wacc[...] = y_total(NZ)
    total = wacc[...]
    for k in range(1, NZ):
        wz_copy(k).wait_recv()
        total = total + zrecv[k].astype(F32)
    wg[...] = total

    @pl.loop(0, H)
    def _(h):
        for o in range(1, C):
            out_copy(h, o).wait_send()
            for t in range(3):
                in_copy(t, h, o).wait_send()
                grad_copy(t, h, o).wait_send()
                grad_copy(t, h, o).wait_recv()

    for o in range(1, C):
        lctx_copy(o).wait_send()
    for o in range(1, NY):
        ly_copy(o).wait_send()
    for k in range(1, NZ):
        lz_copy(k).wait_send()
        wz_copy(k).wait_send()
    for n in range(NCH):
        for o in range(X):
            res_copy(n, o).wait_send()
        for o in range(1, X):
            relay_copy(n, o).wait_send()

    @pl.loop(1, NZ + 1)
    def _(k):
        for o in range(1, NY):
            wy_copy(o, k).wait_send()

    for t in range(3):
        own_grad(t).wait()


def place_kernel(*refs):
    sources, results, held = refs[:4], refs[4:8], refs[8:12]
    in_sem, out_sem = refs[12:]
    pairs = []
    for a in range(4):
        pieces = 4 if sources[a].shape[0] % 64 == 0 else 1
        part = sources[a].shape[0] // pieces
        for j in range(pieces):
            where = pl.ds(j * part, part)
            slot = held[a].at[where, :]
            pairs.append((
                pltpu.make_async_copy(sources[a].at[where, :], slot, in_sem.at[a, j]),
                pltpu.make_async_copy(slot, results[a].at[where, :], out_sem.at[a, j]),
            ))
    for load, store in pairs:
        load.start()
    for load, store in pairs:
        load.wait()
        store.start()
    for load, store in pairs:
        store.wait()


def on_device(
    query_rows, key_rows, value_rows, target, w_out, clip_lengths, timesteps, tile_pattern, tau_prev
):
    RB, DA = query_rows.shape
    C = lax.axis_size("ctx")
    DP = lax.axis_size("dp")
    NY = 2 ** ((DP.bit_length() - 1) // 2)
    NZ = DP // NY
    PR, WD, B = RB * C, DA // C, OUT // DP
    H, X, NCH = WD // HD, C // 2, OUT // CHUNK
    dma = pltpu.SemaphoreType.DMA
    vm = pltpu.VMEM
    anyspec = pl.BlockSpec(memory_space=pl.ANY)
    smem = pl.BlockSpec(memory_space=pltpu.SMEM)
    rows_shape = jax.ShapeDtypeStruct((RB, DA), BF16)
    scratch = [
        vm((PR, WD), BF16), vm((PR, WD), BF16), vm((PR, WD), BF16),
        vm((PR, PR), F32), vm((H, PR, PR), F32), vm((PR, WD), BF16), vm((PR, WD), BF16),
        vm((RB, DA), BF16), vm((DA, OUT), BF16), vm((RB, OUT), BF16), vm((PR, OUT), BF16),
        vm((PR, WD), F32), vm((PR, WD), BF16),
        vm((PR, WD), BF16), vm((PR, WD), BF16), vm((PR, WD), BF16),
        vm((OUT, WD), BF16), vm((NY, NZ, B, WD), BF16), vm((NZ, B, WD), BF16),
        vm((NZ, B, WD), BF16), vm((B, WD), F32),
        vm((3, 8, 128), F32), vm((C, 8, 128), F32), vm((NY, 8, 128), F32), vm((NZ, 8, 128), F32),
        dma((5,)), dma((3, H, C)), dma((3, H, C)), dma((H, C)), dma((H, C)),
        dma((C,)), dma((C,)), dma((NY,)), dma((NY,)), dma((NZ,)), dma((NZ,)),
        dma((NCH, X)), dma((NCH, X)), dma((NCH, X)), dma((NCH, X)),
        dma((NY, NZ)), dma((NY, NZ)), dma((NZ,)), dma((NZ,)),
        dma((3, H, C)), dma((3, H, C)), dma((3,)),
    ]
    shapes = (rows_shape, rows_shape, rows_shape, jax.ShapeDtypeStruct((B, WD), F32))
    results = pl.pallas_call(
        functools.partial(kernel, C, NY, NZ, RB, DA),
        out_shape=shapes,
        in_specs=[anyspec] * 5 + [smem] * 4,
        out_specs=(anyspec, anyspec, anyspec, pl.BlockSpec(memory_space=pltpu.VMEM)),
        scratch_shapes=scratch,
        compiler_params=pltpu.CompilerParams(
            collective_id=0, has_side_effects=True, vmem_limit_bytes=56 * 1024 * 1024
        ),
    )(query_rows, key_rows, value_rows, target, w_out, clip_lengths, timesteps, tile_pattern,
      tau_prev)
    query_grad, key_grad, value_grad, weight_grad = pl.pallas_call(
        place_kernel,
        out_shape=shapes,
        in_specs=[anyspec] * 4,
        out_specs=(anyspec,) * 4,
        scratch_shapes=[
            vm((RB, DA), BF16), vm((RB, DA), BF16), vm((RB, DA), BF16), vm((B, WD), F32),
            dma((4, 4)), dma((4, 4)),
        ],
        compiler_params=pltpu.CompilerParams(vmem_limit_bytes=56 * 1024 * 1024),
    )(*results)
    return query_grad, key_grad, value_grad, weight_grad.T


def solution(mesh):
    return jax.shard_map(
        on_device,
        mesh=mesh,
        in_specs=(
            P(("dp", "ctx"), None),
            P(("dp", "ctx"), None),
            P(("dp", "ctx"), None),
            P(("dp", "ctx"), None),
            P(),
            P("dp", None),
            P("dp", None),
            P("dp", None, None),
            P(),
        ),
        out_specs=(
            P(("dp", "ctx"), None),
            P(("dp", "ctx"), None),
            P(("dp", "ctx"), None),
            P("ctx", "dp"),
        ),
        check_vma=False,
    )
```

```python
import functools
import math

import jax
import jax.numpy as jnp
from jax import lax
from jax.experimental import pallas as pl
from jax.experimental.pallas import tpu as pltpu
from jax.sharding import PartitionSpec as P

HD = 128
OUT = 1536
CLIPS = 4
TILE = 128
MOMENTUM = 0.9
F32 = jnp.float32
BF16 = jnp.bfloat16
CHUNK = 512


def dot_nt(a, b):
    return lax.dot_general(a, b, (((1,), (1,)), ((), ())), preferred_element_type=F32)


def dot_nn(a, b):
    return jnp.dot(a, b, preferred_element_type=F32)


def dot_tn(a, b):
    return lax.dot_general(a, b, (((0,), (0,)), ((), ())), preferred_element_type=F32)


def superloss_weight(clip_loss, tau_now):
    argument = jnp.maximum(-0.3, 0.5 * (clip_loss - tau_now))
    branch = jnp.log1p(argument)
    for sweep in range(5):
        exp_value = jnp.exp(branch)
        branch = branch - (branch * exp_value - argument) / (exp_value * (branch + 1.0))
    return jnp.exp(-branch)


def kernel(
    C, NY, NZ, RB, DA,
    q_in, k_in, v_in, tgt_in, w_in, len_s, time_s, pat_s, tau_s,
    qg, kg, vg, wg,
    qh, kh, vh, bias, probs, oh, osc, orow, w_v, tgt_v, respack, graw, gh,
    dqh, dkh, dvh, wt, yrecv, zsend, zrecv, wacc, lsend, lctx, ly, lz,
    local_sem, in_send, in_recv, out_send, out_recv, lc_send, lc_recv, ly_send, ly_recv,
    lz_send, lz_recv, res_send, res_recv, rel_send, rel_recv, wy_send, wy_recv, wz_send, wz_recv,
    gr_send, gr_recv, own_sem,
):
    PR = RB * C
    WD = DA // C
    H = WD // HD
    X = C // 2
    DP = NY * NZ
    B = OUT // DP
    NT = PR // TILE
    NCH = OUT // CHUNK
    me = lax.axis_index("ctx")
    dp = lax.axis_index("dp")
    xi, core = me // 2, lax.rem(me, 2)
    zi, yi = dp // NY, lax.rem(dp, NY)
    sib = xi * 2 + (1 - core)

    def ctx_peer(o):
        return lax.rem(me + o, C)

    def ctx_src(o):
        return lax.rem(me + C - o, C)

    def x_peer(o):
        return lax.rem(xi + o, X) * 2 + core

    def y_dev(o):
        return zi * NY + lax.rem(yi + o, NY)

    def z_dev(k):
        return lax.rem(zi + k, NZ) * NY + yi

    def rows(p, n=RB):
        return pl.ds(pl.multiple_of(p * n, n), n)

    def cols(base, h):
        return pl.ds(pl.multiple_of(base + h * HD, HD), HD)

    def remote(src, dst, ss, rs, where):
        return pltpu.make_async_remote_copy(
            src_ref=src, dst_ref=dst, send_sem=ss, recv_sem=rs,
            device_id=where, device_id_type=pl.DeviceIdType.MESH,
        )

    ins, heads_in = (q_in, k_in, v_in), (qh, kh, vh)
    grads_h, grads_out = (dqh, dkh, dvh), (qg, kg, vg)

    def local_in(t):
        return pltpu.make_async_copy(
            ins[t].at[:, pl.ds(pl.multiple_of(me * WD, WD), WD)], heads_in[t].at[rows(me), :],
            local_sem.at[t])

    copy_t = pltpu.make_async_copy(tgt_in, tgt_v, local_sem.at[3])
    copy_w = pltpu.make_async_copy(w_in, w_v, local_sem.at[4])
    for t in range(3):
        local_in(t).start()
    copy_t.start()
    copy_w.start()

    barrier = pltpu.get_barrier_semaphore()
    for o in range(1, C):
        pl.semaphore_signal(barrier, inc=1, device_id={"ctx": ctx_peer(o)},
                            device_id_type=pl.DeviceIdType.MESH)
    for o in range(1, NY):
        pl.semaphore_signal(barrier, inc=1, device_id={"dp": y_dev(o)},
                            device_id_type=pl.DeviceIdType.MESH)
    for k in range(1, NZ):
        pl.semaphore_signal(barrier, inc=1, device_id={"dp": z_dev(k)},
                            device_id_type=pl.DeviceIdType.MESH)
    pl.semaphore_wait(barrier, (C - 1) + (NY - 1) + (NZ - 1))

    def in_copy(t, h, o):
        p = ctx_peer(o)
        return remote(ins[t].at[:, cols(p * WD, h)], heads_in[t].at[rows(me), cols(0, h)],
                      in_send.at[t, h, o], in_recv.at[t, h, o], {"ctx": p})

    @pl.loop(0, H)
    def _(h):
        for o in range(1, C):
            for t in range(3):
                in_copy(t, h, o).start()

    ends = []
    for c in range(CLIPS):
        ends.append(len_s[0, c] if c == 0 else ends[-1] + len_s[0, c])

    def clip_of(pos):
        total = (pos >= ends[0]).astype(jnp.int32)
        for c in range(1, CLIPS):
            total = total + (pos >= ends[c]).astype(jnp.int32)
        return total

    @pl.loop(0, NT)
    def _(i):
        rpos = lax.broadcasted_iota(jnp.int32, (TILE, PR), 0) + i * TILE
        cpos = lax.broadcasted_iota(jnp.int32, (TILE, PR), 1)
        tile = cpos // TILE
        ok = (tile == i).astype(jnp.int32)
        for j in range(NT):
            ok = jnp.where(tile == j, jnp.maximum(ok, pat_s[0, i, j]), ok)
        allowed = (clip_of(rpos) == clip_of(cpos)) & (ok > 0)
        bias[rows(i, TILE), :] = jnp.where(allowed, 0.0, -1e30)

    scale = 1.0 / math.sqrt(HD)
    for t in range(3):
        local_in(t).wait()

    def out_copy(h, o):
        p = ctx_peer(o)
        return remote(oh.at[rows(p), cols(0, h)], orow.at[:, cols(me * WD, h)],
                      out_send.at[h, o], out_recv.at[h, o], {"ctx": p})

    @pl.loop(0, H)
    def _(h):
        for o in range(1, C):
            for t in range(3):
                in_copy(t, h, o).wait_recv()
        k = kh[:, cols(0, h)]
        v = vh[:, cols(0, h)]
        for i in range(NT):
            rr = slice(i * TILE, (i + 1) * TILE)
            s = dot_nt(qh[rr, cols(0, h)], k) * scale + bias[rr, :]
            e = jnp.exp(s - jnp.max(s, axis=1, keepdims=True))
            p = e * (1.0 / jnp.sum(e, axis=1, keepdims=True))
            probs[h, rr, :] = p
            oh[rr, cols(0, h)] = dot_nn(p.astype(BF16), v).astype(BF16)
        for o in range(1, C):
            out_copy(h, o).start()
        orow[:, cols(me * WD, h)] = oh[rows(me), cols(0, h)]

    copy_t.wait()
    copy_w.wait()

    def partial_pred(n, low, high):
        total = None
        for c in range(C):
            part_rows = slice(c * WD + low * HD, c * WD + high * HD)
            term = dot_nn(orow[:, part_rows], w_v[part_rows, n * CHUNK:(n + 1) * CHUNK])
            total = term if total is None else total + term
        return total

    half = max(H // 2, 1)

    @pl.loop(0, half)
    def _(h):
        for o in range(1, C):
            out_copy(h, o).wait_recv()

    early = [partial_pred(n, 0, half) for n in range(NCH)]

    @pl.loop(half, H)
    def _(h):
        for o in range(1, C):
            out_copy(h, o).wait_recv()

    def res_view(p, n):
        return respack.at[rows(p), pl.ds(n * CHUNK, CHUNK)]

    def res_copy(n, o):
        p = sib if o == 0 else x_peer(o)
        return remote(res_view(me, n), res_view(me, n), res_send.at[n, o], res_recv.at[n, o],
                      {"ctx": p})

    def relay_copy(n, o):
        p = lax.rem(xi + X - o, X) * 2 + core
        return remote(res_view(p, n), res_view(p, n), rel_send.at[n, o], rel_recv.at[n, o],
                      {"ctx": sib})

    rowsq = jnp.zeros((RB, 1), F32)
    for n in range(NCH):
        cc = slice(n * CHUNK, (n + 1) * CHUNK)
        res = early[n] - tgt_v[:, cc].astype(F32)
        if half < H:
            res = res + partial_pred(n, half, H)
        rowsq = rowsq + jnp.sum(res * res, axis=1, keepdims=True)
        respack[rows(me), cc] = res.astype(BF16)
        if n < NCH - 1:
            for o in range(1, X):
                res_copy(n, o).start()

    lane = lax.broadcasted_iota(jnp.int32, (RB, 128), 1)
    own_clip = clip_of(lax.broadcasted_iota(jnp.int32, (RB, 128), 0) + me * RB)
    part = jnp.sum(jnp.where(own_clip == lane, rowsq, 0.0), axis=0, keepdims=True)
    lsend[0] = jnp.broadcast_to(part, (8, 128))

    def lctx_copy(o):
        return remote(lsend.at[0], lctx.at[o], lc_send.at[o], lc_recv.at[o], {"ctx": ctx_peer(o)})

    def ly_copy(o):
        return remote(lsend.at[1], ly.at[o], ly_send.at[o], ly_recv.at[o], {"dp": y_dev(o)})

    def lz_copy(k):
        return remote(lsend.at[2], lz.at[k], lz_send.at[k], lz_recv.at[k], {"dp": z_dev(k)})

    for o in range(1, C):
        lctx_copy(o).start()

    for o in range(1, X):
        res_copy(NCH - 1, o).start()
    for n in range(NCH):
        res_copy(n, 0).start()

    def grad_rows(p):
        graw[rows(p), :] = dot_nt(respack[rows(p), :], w_v[rows(me, WD), :])

    grad_rows(me)
    lanes8 = lax.broadcasted_iota(jnp.int32, (8, 128), 1)
    length = jnp.ones((8, 128), F32)
    weight = jnp.zeros((8, 128), F32)
    for c in range(CLIPS):
        length = jnp.where(lanes8 == c, len_s[0, c].astype(F32), length)
        weight = jnp.where(lanes8 == c, 1.0 + time_s[0, c].astype(F32) / 250.0, weight)
    clip_sq = lsend[0]
    for o in range(1, C):
        lctx_copy(o).wait_recv()
        clip_sq = clip_sq + lctx[o]
    clip_loss = weight * clip_sq / (length * OUT)
    loss_sum = jnp.broadcast_to(jnp.sum(clip_loss, axis=1, keepdims=True), (8, 128))
    lsend[1] = loss_sum
    for o in range(1, NY):
        ly_copy(o).start()

    for n in range(NCH):
        res_copy(n, 0).wait_recv()
    grad_rows(sib)
    for o in range(1, NY):
        ly_copy(o).wait_recv()
        loss_sum = loss_sum + ly[o]
    lsend[2] = loss_sum
    for k in range(1, NZ):
        lz_copy(k).start()

    for n in range(NCH):
        for o in range(1, X):
            res_copy(n, o).wait_recv()
            relay_copy(n, o).start()
    for o in range(1, X):
        grad_rows(lax.rem(xi + X - o, X) * 2 + core)

    for k in range(1, NZ):
        lz_copy(k).wait_recv()
        loss_sum = loss_sum + lz[k]
    tau_now = MOMENTUM * tau_s[0] + (1.0 - MOMENTUM) * (loss_sum / (DP * CLIPS))
    clip_scale = (superloss_weight(clip_loss, tau_now) * weight)[0:1, :]
    norm = 1.0 / math.sqrt(PR * DP)

    def row_scale(i):
        pos = lax.broadcasted_iota(jnp.int32, (RB, 128), 0) + i * RB
        return jnp.sum(jnp.where(clip_of(pos) == lane, clip_scale, 0.0), axis=1, keepdims=True)

    scales = [row_scale(i) for i in range(C)]
    for i in range(C):
        rr = slice(i * RB, (i + 1) * RB)
        osc[rr, :] = (oh[rr, :].astype(F32) * (scales[i] * norm)).astype(BF16)

    for n in range(NCH):
        for o in range(1, X):
            relay_copy(n, o).wait_recv()
    def weight_rows(n, width):
        wt[rows(n, width), :] = dot_tn(respack[:, rows(n, width)], osc[...]).astype(BF16)

    def wy_copy(o, k):
        kk = lax.rem(zi + k, NZ)
        return remote(wt.at[rows(kk * NY + lax.rem(yi + o, NY), B), :], yrecv.at[o, lax.rem(k, NZ)],
                      wy_send.at[o, lax.rem(k, NZ)], wy_recv.at[o, lax.rem(k, NZ)],
                      {"dp": y_dev(o)})

    def wz_copy(k):
        return remote(zsend.at[k], zrecv.at[k], wz_send.at[k], wz_recv.at[k], {"dp": z_dev(k)})

    def y_total(k):
        total = wt[rows(lax.rem(zi + k, NZ) * NY + yi, B), :].astype(F32)
        for o in range(1, NY):
            wy_copy(o, k).wait_recv()
            total = total + yrecv[o, lax.rem(k, NZ)].astype(F32)
        return total

    by_z = (NY * B) % 128 == 0
    if not by_z:
        pl.loop(0, OUT // 256)(lambda n: weight_rows(n, 256))

    @pl.loop(1, NZ + 1)
    def _(k):
        if by_z:
            weight_rows(lax.rem(zi + k, NZ), NY * B)
        for o in range(1, NY):
            wy_copy(o, k).start()

    for o in range(1, X):
        grad_rows(lax.rem(xi + X - o, X) * 2 + (1 - core))
    for i in range(C):
        rr = slice(i * RB, (i + 1) * RB)
        gh[rr, :] = (graw[rr, :] * scales[i]).astype(BF16)


    def grad_copy(t, h, o):
        p = ctx_peer(o)
        return remote(grads_h[t].at[rows(p), cols(0, h)], grads_out[t].at[:, cols(me * WD, h)],
                      gr_send.at[t, h, o], gr_recv.at[t, h, o], {"ctx": p})

    def own_grad(t):
        return pltpu.make_async_copy(
            grads_h[t].at[rows(me), :],
            grads_out[t].at[:, pl.ds(pl.multiple_of(me * WD, WD), WD)], own_sem.at[t])

    per_head = -(-NZ // H)

    @pl.loop(0, H)
    def _(h):
        hc = cols(0, h)
        k = kh[:, hc]
        v = vh[:, hc]
        dk_t = jnp.zeros((HD, PR), F32)
        dv_t = jnp.zeros((HD, PR), F32)
        for i in range(NT):
            rr = slice(i * TILE, (i + 1) * TILE)
            g = gh[rr, hc]
            p = probs[h, rr, :]
            gf = g.astype(F32)
            delta = jnp.sum(gf * oh[rr, hc].astype(F32), axis=1, keepdims=True)
            ds = (p * (dot_nt(g, v) - delta)).astype(BF16)
            dqh[rr, hc] = (dot_nn(ds, k) * scale).astype(BF16)
            dk_t = dk_t + dot_nn(qh[rr, hc].T, ds)
            dv_t = dv_t + dot_nn(g.T, p.astype(BF16))
        dkh[:, hc] = (dk_t * scale).T.astype(BF16)
        dvh[:, hc] = dv_t.T.astype(BF16)
        for o in range(1, C):
            for t in range(3):
                grad_copy(t, h, o).start()
        for kk in range(per_head):
            step = h * per_head + kk + 1

            @pl.when(step < NZ)
            def _():
                zsend[step] = y_total(step).astype(BF16)
                wz_copy(step).start()

    for t in range(3):
        own_grad(t).start()
    wacc[...] = y_total(NZ)
    total = wacc[...]
    for k in range(1, NZ):
        wz_copy(k).wait_recv()
        total = total + zrecv[k].astype(F32)
    wg[...] = total

    @pl.loop(0, H)
    def _(h):
        for o in range(1, C):
            out_copy(h, o).wait_send()
            for t in range(3):
                in_copy(t, h, o).wait_send()
                grad_copy(t, h, o).wait_send()
                grad_copy(t, h, o).wait_recv()

    for o in range(1, C):
        lctx_copy(o).wait_send()
    for o in range(1, NY):
        ly_copy(o).wait_send()
    for k in range(1, NZ):
        lz_copy(k).wait_send()
        wz_copy(k).wait_send()
    for n in range(NCH):
        for o in range(X):
            res_copy(n, o).wait_send()
        for o in range(1, X):
            relay_copy(n, o).wait_send()

    @pl.loop(1, NZ + 1)
    def _(k):
        for o in range(1, NY):
            wy_copy(o, k).wait_send()

    for t in range(3):
        own_grad(t).wait()


def place_kernel(*refs):
    sources, results, held = refs[:4], refs[4:8], refs[8:12]
    in_sem, out_sem = refs[12:]
    pairs = []
    for a in range(4):
        pieces = 4 if sources[a].shape[0] % 64 == 0 else 1
        part = sources[a].shape[0] // pieces
        for j in range(pieces):
            where = pl.ds(j * part, part)
            slot = held[a].at[where, :]
            pairs.append((
                pltpu.make_async_copy(sources[a].at[where, :], slot, in_sem.at[a, j]),
                pltpu.make_async_copy(slot, results[a].at[where, :], out_sem.at[a, j]),
            ))
    for load, store in pairs:
        load.start()
    for load, store in pairs:
        load.wait()
        store.start()
    for load, store in pairs:
        store.wait()


def on_device(
    query_rows, key_rows, value_rows, target, w_out, clip_lengths, timesteps, tile_pattern, tau_prev
):
    RB, DA = query_rows.shape
    C = lax.axis_size("ctx")
    DP = lax.axis_size("dp")
    NY = 2 ** ((DP.bit_length() - 1) // 2)
    NZ = DP // NY
    PR, WD, B = RB * C, DA // C, OUT // DP
    H, X, NCH = WD // HD, C // 2, OUT // CHUNK
    dma = pltpu.SemaphoreType.DMA
    vm = pltpu.VMEM
    anyspec = pl.BlockSpec(memory_space=pl.ANY)
    smem = pl.BlockSpec(memory_space=pltpu.SMEM)
    rows_shape = jax.ShapeDtypeStruct((RB, DA), BF16)
    scratch = [
        vm((PR, WD), BF16), vm((PR, WD), BF16), vm((PR, WD), BF16),
        vm((PR, PR), F32), vm((H, PR, PR), F32), vm((PR, WD), BF16), vm((PR, WD), BF16),
        vm((RB, DA), BF16), vm((DA, OUT), BF16), vm((RB, OUT), BF16), vm((PR, OUT), BF16),
        vm((PR, WD), F32), vm((PR, WD), BF16),
        vm((PR, WD), BF16), vm((PR, WD), BF16), vm((PR, WD), BF16),
        vm((OUT, WD), BF16), vm((NY, NZ, B, WD), BF16), vm((NZ, B, WD), BF16),
        vm((NZ, B, WD), BF16), vm((B, WD), F32),
        vm((3, 8, 128), F32), vm((C, 8, 128), F32), vm((NY, 8, 128), F32), vm((NZ, 8, 128), F32),
        dma((5,)), dma((3, H, C)), dma((3, H, C)), dma((H, C)), dma((H, C)),
        dma((C,)), dma((C,)), dma((NY,)), dma((NY,)), dma((NZ,)), dma((NZ,)),
        dma((NCH, X)), dma((NCH, X)), dma((NCH, X)), dma((NCH, X)),
        dma((NY, NZ)), dma((NY, NZ)), dma((NZ,)), dma((NZ,)),
        dma((3, H, C)), dma((3, H, C)), dma((3,)),
    ]
    shapes = (rows_shape, rows_shape, rows_shape, jax.ShapeDtypeStruct((B, WD), F32))
    results = pl.pallas_call(
        functools.partial(kernel, C, NY, NZ, RB, DA),
        out_shape=shapes,
        in_specs=[anyspec] * 5 + [smem] * 4,
        out_specs=(anyspec, anyspec, anyspec, pl.BlockSpec(memory_space=pltpu.VMEM)),
        scratch_shapes=scratch,
        compiler_params=pltpu.CompilerParams(
            collective_id=0, has_side_effects=True, vmem_limit_bytes=56 * 1024 * 1024
        ),
    )(query_rows, key_rows, value_rows, target, w_out, clip_lengths, timesteps, tile_pattern,
      tau_prev)
    query_grad, key_grad, value_grad, weight_grad = pl.pallas_call(
        place_kernel,
        out_shape=shapes,
        in_specs=[anyspec] * 4,
        out_specs=(anyspec,) * 4,
        scratch_shapes=[
            vm((RB, DA), BF16), vm((RB, DA), BF16), vm((RB, DA), BF16), vm((B, WD), F32),
            dma((4, 4)), dma((4, 4)),
        ],
        compiler_params=pltpu.CompilerParams(vmem_limit_bytes=56 * 1024 * 1024),
    )(*results)
    return query_grad, key_grad, value_grad, weight_grad.T


def solution(mesh):
    return jax.shard_map(
        on_device,
        mesh=mesh,
        in_specs=(
            P(("dp", "ctx"), None),
            P(("dp", "ctx"), None),
            P(("dp", "ctx"), None),
            P(("dp", "ctx"), None),
            P(),
            P("dp", None),
            P("dp", None),
            P("dp", None, None),
            P(),
        ),
        out_specs=(
            P(("dp", "ctx"), None),
            P(("dp", "ctx"), None),
            P(("dp", "ctx"), None),
            P("ctx", "dp"),
        ),
        check_vma=False,
    )
```
